32 devices in a mesh: ctx: 8 (over y, x, core), wsh: 4 (over z).
Axes of the slice: x: 2, y: 2, z: 4, core: 2. Of those that a mesh axis runs over, the one named last changes fastest.
Arguments:
- block_input: bfloat16 [8, 1024, 768], P('wsh', 'ctx'), may hold values from -6 to 6
- ln1_gain: bfloat16 [768], P('wsh'), may hold values from 0.5 to 1.5
- ln1_bias: bfloat16 [768], P('wsh'), may hold values from -4 to 4
- w_qkv: bfloat16 [768, 2304], P('wsh'), may hold values from -0.21875 to 0.21875
- bias_query: bfloat16 [768], P('wsh'), may hold values from -4 to 4
- bias_value: bfloat16 [768], P('wsh'), may hold values from -1.5 to 1.5
- w_out: bfloat16 [768, 768], P('wsh'), may hold values from -6 to 6
- bias_out: bfloat16 [768], P('wsh'), may hold values from -4 to 4
- ln2_gain: bfloat16 [768], P('wsh'), may hold values from 0.5 to 1.5
- ln2_bias: bfloat16 [768], P('wsh'), may hold values from -4 to 4
- w_up: bfloat16 [768, 3072], P('wsh'), may hold values from -0.21875 to 0.21875
- bias_up: bfloat16 [3072], P('wsh'), may hold values from -6 to 6
- w_down: bfloat16 [3072, 768], P('wsh'), may hold values from -0.109375 to 0.109375
- bias_down: bfloat16 [768], P('wsh'), may hold values from -4 to 4
- pair_of_device: int32 [8], replicated, may hold values from 0 to 7, each once
- cotangent: bfloat16 [8, 1024, 768], P('wsh', 'ctx'), may hold values from -6 to 6
Outputs:
- output: bfloat16 [8, 1024, 768], P('wsh', 'ctx')
- grad_input: float32 [8, 1024, 768], P('wsh', 'ctx')
- grad_ln1_gain: float32 [768], P('wsh')
- grad_ln1_bias: float32 [768], P('wsh')
- grad_qkv: float32 [768, 2304], P('wsh')
- grad_bias_query: float32 [768], P('wsh')
- grad_bias_value: float32 [768], P('wsh')
- grad_out: float32 [768, 768], P('wsh')
- grad_bias_out: float32 [768], P('wsh')
- grad_ln2_gain: float32 [768], P('wsh')
- grad_ln2_bias: float32 [768], P('wsh')
- grad_up: float32 [768, 3072], P('wsh')
- grad_bias_up: float32 [3072], P('wsh')
- grad_down: float32 [3072, 768], P('wsh')
- grad_bias_down: float32 [768], P('wsh')
The draws below stay inside these ranges and needn't reach their ends.
Inputs may be any that keep to these rules, and one draw needn't show every extreme that they name: Each of 0 to 7 appears once; device i of ctx holds, for each of its sequences, the blocks pair_of_device[i] and 15 - pair_of_device[i] of 64 tokens, the lower one first.
All inputs are finite; a program needn't handle non-finite values.
Results may differ from the reference program's by a relative error of at most 0.017.
Values may be sent and summed in bfloat16 or wider, within the bound.
A program may use at most 384 MiB of HBM per device.

```python
import math
import jax
import jax.numpy as jnp
from jax import lax

D = 768
HEADS = 12
HD = 64
FF = 3072
BLK = 64
SEQLEN = 1024
SEQS = 8
N_CTX = 8


def level_of(stream_key, shape, pieces, least, high):
    level = 1.0
    for dim, blocks in pieces:
        draws = jax.random.uniform(jax.random.fold_in(jax.random.fold_in(stream_key, 6), dim), (blocks,), jnp.float32, least / len(pieces), high / len(pieces))
        level = level * jnp.repeat(jnp.exp(draws), shape[dim] // blocks).reshape((-1,) + (1,) * (len(shape) - 1 - dim))
    return level


def scatter_about(stream_key, dims, width, limit, pieces=(), kind=jnp.bfloat16):
    values = jax.random.normal(stream_key, dims, jnp.float32) * width
    if len(pieces) > 0:
        values = level_of(stream_key, dims, pieces, -0.22, 0.18) * values
    return jnp.clip(values, min=-limit, max=limit).astype(kind)


def setup_inputs(seed: int = 0) -> dict:
    splits = jax.random.split(jax.random.key(seed), 17)
    block_input = scatter_about(splits[0], (SEQS, SEQLEN, D), 1.0, 6.0, ((0, 4), (1, 8)))
    ln1_gain = jnp.clip(1.0 + 0.1 * jax.random.normal(splits[1], (D,), jnp.float32), 0.5, 1.5).astype(jnp.bfloat16)
    ln1_bias = scatter_about(splits[2], (D,), 0.3, 4.0, ((0, 4),))
    w_qkv = scatter_about(splits[3], (D, 3 * D), D ** -0.5, 0.21875, ((0, 4),))
    bias_query = scatter_about(splits[4], (D,), 0.3, 4.0, ((0, 4),))
    bias_value = scatter_about(splits[5], (D,), 0.1, 1.5, ((0, 4),))
    w_out = scatter_about(splits[6], (D, D), 1 ** -0.5, 6.0, ((0, 4),))
    bias_out = scatter_about(splits[7], (D,), 0.3, 4.0, ((0, 4),))
    ln2_gain = jnp.clip(1.0 + 0.1 * jax.random.normal(splits[8], (D,), jnp.float32), 0.5, 1.5).astype(jnp.bfloat16)
    ln2_bias = scatter_about(splits[9], (D,), 0.3, 4.0, ((0, 4),))
    w_up = scatter_about(splits[10], (D, FF), D ** -0.5, 0.21875, ((0, 4),))
    bias_up = scatter_about(splits[11], (FF,), 0.5, 6.0, ((0, 4),))
    w_down = scatter_about(splits[12], (FF, D), FF ** -0.5, 0.109375, ((0, 4),))
    bias_down = scatter_about(splits[13], (D,), 0.3, 4.0, ((0, 4),))
    pair_of_device = jax.random.permutation(splits[14], N_CTX).astype(jnp.int32)
    cotangent = scatter_about(splits[15], (SEQS, SEQLEN, D), 1.0, 6.0, ((0, 4), (1, 8)))
    return {"block_input": block_input, "ln1_gain": ln1_gain, "ln1_bias": ln1_bias, "w_qkv": w_qkv, "bias_query": bias_query, "bias_value": bias_value, "w_out": w_out, "bias_out": bias_out, "ln2_gain": ln2_gain, "ln2_bias": ln2_bias, "w_up": w_up, "bias_up": bias_up, "w_down": w_down, "bias_down": bias_down, "pair_of_device": pair_of_device, "cotangent": cotangent}


EPSILON = 1e-05
MASKED = -1000000000.0
HIGHEST = lax.Precision.HIGHEST

@jax.custom_vjp
def low(v):
    return lax.optimization_barrier(v.astype(jnp.bfloat16)).astype(jnp.float32)

@jax.custom_vjp
def low_back(v):
    return v

def low_keep(v):
    return (low(v), None)

def low_pass(kept, grad):
    return (grad,)

def back_keep(v):
    return (v, None)

def back_low(kept, grad):
    return (low(grad),)
low.defvjp(low_keep, low_pass)
low_back.defvjp(back_keep, back_low)

def layer_norm(values, gain, shift):
    center = lax.optimization_barrier(jnp.mean(values, axis=-1, keepdims=True))
    offset = values - center
    spread = lax.optimization_barrier(jnp.mean(offset * offset, axis=-1, keepdims=True))
    return offset * lax.rsqrt(spread + EPSILON) * gain + shift

def token_positions(pair_of_device):
    row_index = jnp.arange(SEQLEN, dtype=jnp.int32)
    owner = (row_index // (2 * BLK)).astype(jnp.int32)
    inner = (row_index % (2 * BLK)).astype(jnp.int32)
    paired = jnp.take(pair_of_device, owner)
    which = jnp.where(inner < BLK, paired, 2 * N_CTX - 1 - paired)
    return (which * BLK + inner % BLK).astype(jnp.int32)

def attention(queries, keys, values, positions):
    group = queries.shape[0]
    query_len = math.gcd(512, SEQLEN)
    scale = HD ** (-0.5)

    def one_block(inputs):
        query_block, query_pos = inputs
        scores = jnp.einsum('gqhd,gkhd->ghqk', query_block, keys, precision=HIGHEST) * scale
        scores = low_back(scores)
        scores = jnp.where(positions[None, None, None, :] <= query_pos[None, None, :, None], scores, MASKED)
        shifted = scores - lax.optimization_barrier(jnp.max(scores, axis=-1, keepdims=True))
        weights = jnp.exp(shifted)
        probs = weights / lax.optimization_barrier(jnp.sum(weights, axis=-1, keepdims=True))
        return jnp.einsum('ghqk,gkhd->gqhd', low(probs), values, precision=HIGHEST)
    blocks = jnp.moveaxis(queries.reshape(group, SEQLEN // query_len, query_len, HEADS, HD), 1, 0)
    spots = positions.reshape(SEQLEN // query_len, query_len)
    result = lax.map(jax.checkpoint(one_block), (blocks, spots))
    return jnp.moveaxis(result, 0, 1).reshape(group, SEQLEN, D)

def block_forward(slab, params, positions):
    gain_first, shift_first, weight_qkv, query_shift, value_shift, weight_out, out_shift, gain_second, shift_second, weight_up, up_shift, weight_down, down_shift = params
    group = slab.shape[0]
    normed = low(layer_norm(slab, gain_first, shift_first))
    qkv_shift = jnp.concatenate([query_shift, jnp.zeros_like(query_shift), value_shift])
    qkv = low_back(low(jnp.einsum('gsd,de->gse', normed, weight_qkv, precision=HIGHEST) + qkv_shift))
    queries = qkv[..., :D].reshape(group, SEQLEN, HEADS, HD)
    keys = qkv[..., D:2 * D].reshape(group, SEQLEN, HEADS, HD)
    values = qkv[..., 2 * D:].reshape(group, SEQLEN, HEADS, HD)
    attended = low_back(low(attention(queries, keys, values, positions)))
    branch = low_back(jnp.einsum('gsd,de->gse', attended, weight_out, precision=HIGHEST) + out_shift)
    middle = slab + branch
    normed_two = low(layer_norm(middle, gain_second, shift_second))
    hidden = low_back(jnp.einsum('gsd,df->gsf', normed_two, weight_up, precision=HIGHEST) + up_shift)
    active = low(jax.nn.gelu(hidden, approximate=True))
    return middle + jnp.einsum('gsf,fd->gsd', active, weight_down, precision=HIGHEST) + down_shift

def reference(block_input, ln1_gain, ln1_bias, w_qkv, bias_query, bias_value, w_out, bias_out, ln2_gain, ln2_bias, w_up, bias_up, w_down, bias_down, pair_of_device, cotangent):
    positions = token_positions(pair_of_device)
    group = math.gcd(SEQS, max(1, 4096 // SEQLEN))
    params = (ln1_gain.astype(jnp.float32), ln1_bias.astype(jnp.float32), w_qkv.astype(jnp.float32), bias_query.astype(jnp.float32), bias_value.astype(jnp.float32), w_out.astype(jnp.float32), bias_out.astype(jnp.float32), ln2_gain.astype(jnp.float32), ln2_bias.astype(jnp.float32), w_up.astype(jnp.float32), bias_up.astype(jnp.float32), w_down.astype(jnp.float32), bias_down.astype(jnp.float32))

    def forward(inputs, weights):
        stacked = inputs.reshape(SEQS // group, group, SEQLEN, D)

        def visit(running, slab):
            return (running, block_forward(slab, weights, positions))
        ignored, outputs = lax.scan(visit, None, stacked)
        return outputs.reshape(SEQS, SEQLEN, D)
    output, pullback = jax.vjp(forward, block_input.astype(jnp.float32), params)
    input_grad, grads = pullback(cotangent.astype(jnp.float32))
    return (output.astype(jnp.bfloat16), input_grad, grads[0], grads[1], grads[2], grads[3], grads[4], grads[5], grads[6], grads[7], grads[8], grads[9], grads[10], grads[11], grads[12])
```

```python
import functools
import math

import jax
import jax.numpy as jnp
from jax import lax
from jax.experimental import pallas as pl
from jax.experimental.pallas import tpu as pltpu
from jax.sharding import PartitionSpec as P

HEADS = 12


EPSILON = 1e-05
MASKED = -1000000000.0
LOWEST = -1e30


def layer_norm(values, gain, shift):
    center = jnp.mean(values, axis=-1, keepdims=True)
    offset = values - center
    spread = jnp.mean(offset * offset, axis=-1, keepdims=True)
    return offset * lax.rsqrt(spread + EPSILON) * gain + shift


def gelu_tanh(values):
    return jax.nn.gelu(values, approximate=True)


def key_positions(row_index, pair_table, block_len):
    places = pair_table.shape[0]
    owner = row_index // (2 * block_len)
    inner = row_index % (2 * block_len)
    hits = owner[:, None] == jnp.arange(places, dtype=jnp.int32)[None, :]
    chosen = jnp.sum(jnp.where(hits, pair_table[None, :], 0), axis=1)
    which = jnp.where(inner < block_len, chosen, 2 * places - 1 - chosen)
    return which * block_len + inner % block_len


def lower_rows(array, block_len):
    seq_count, row_total, feature = array.shape
    paired = array.reshape(seq_count, row_total // (2 * block_len), 2, block_len, feature)
    return paired[:, :, 0].reshape(seq_count, row_total // 2, feature)


def lower_spots(spots, block_len):
    return spots.reshape(-1, 2, block_len)[:, 0].reshape(-1)


def online_step(state, query, query_pos, keys, values, key_pos, scale):
    accum, top_score, total = state
    scores = jnp.einsum("sqhd,skhd->shqk", query, keys, preferred_element_type=jnp.float32) * scale
    scores = jnp.where(
        key_pos[None, None, None, :] <= query_pos[None, None, :, None], scores, MASKED
    )
    new_top = jnp.maximum(top_score, jnp.max(scores, axis=-1))
    fading = jnp.exp(top_score - new_top)
    weights = jnp.exp(scores - new_top[..., None])
    total = total * fading + jnp.sum(weights, axis=-1)
    accum = accum * fading[..., None] + jnp.einsum(
        "shqk,skhd->shqd", weights.astype(jnp.bfloat16), values, preferred_element_type=jnp.float32
    )
    return (accum, new_top, total)


def scores_back(query, query_pos, log_total, delta, grad_head, keys, values, key_pos, scale):
    scores = jnp.einsum("sqhd,skhd->shqk", query, keys, preferred_element_type=jnp.float32) * scale
    scores = jnp.where(
        key_pos[None, None, None, :] <= query_pos[None, None, :, None], scores, MASKED
    )
    probs = jnp.exp(scores - log_total[..., None])
    grad_probs = jnp.einsum(
        "sqhd,skhd->shqk", grad_head, values, preferred_element_type=jnp.float32
    )
    grad_scores = (probs * (grad_probs - delta[..., None])).astype(jnp.bfloat16)
    return (probs.astype(jnp.bfloat16), grad_scores)


CHUNK = 256


def to_natural(order_ref, source_ref, target_ref, block_len):
    for block in range(source_ref.shape[0] // block_len):
        start = pl.multiple_of(order_ref[block] * block_len, block_len)
        target_ref[pl.ds(block * block_len, block_len), :] = source_ref[pl.ds(start, block_len), :]


def from_natural(order_ref, source_ref, target_ref, block_len):
    for block in range(source_ref.shape[0] // block_len):
        start = pl.multiple_of(order_ref[block] * block_len, block_len)
        target_ref[pl.ds(start, block_len), :] = source_ref[pl.ds(block * block_len, block_len), :]


def causal_scores(query, keys, first):
    scores = lax.dot_general(
        query, keys, (((1,), (1,)), ((), ())), preferred_element_type=jnp.float32
    )
    rows = lax.broadcasted_iota(jnp.int32, scores.shape, 0) + first
    columns = lax.broadcasted_iota(jnp.int32, scores.shape, 1)
    return jnp.where(columns <= rows, scores, MASKED)


def attend_kernel(head_size, block_len, order_ref, x_ref, out_ref, exact_ref, lse_ref, rows_ref, near_ref):
    total, width = x_ref.shape
    group = width // 3
    chunk = min(CHUNK, total)
    scale = head_size ** (-0.5)
    to_natural(order_ref, x_ref, rows_ref, block_len)
    for head in range(group // head_size):
        spot = head * head_size
        for first in range(0, total, chunk):
            last = first + chunk
            query = rows_ref[first:last, spot : spot + head_size] * jnp.bfloat16(scale)
            keys = rows_ref[:last, group + spot : group + spot + head_size]
            values = rows_ref[:last, 2 * group + spot : 2 * group + spot + head_size]
            scores = causal_scores(query, keys, first)
            top = jnp.max(scores, axis=1, keepdims=True)
            weights = jnp.exp(scores - top)
            amount = jnp.sum(weights, axis=1, keepdims=True)
            mixed = jnp.dot(
                weights.astype(jnp.bfloat16), values, preferred_element_type=jnp.float32
            ) * (1.0 / amount)
            exact_ref[first:last, spot : spot + head_size] = mixed
            near_ref[first:last, spot : spot + head_size] = mixed.astype(jnp.bfloat16)
            lse_ref[first:last, head : head + 1] = top + jnp.log(amount)
    from_natural(order_ref, near_ref, out_ref, block_len)


def attend_back_kernel(
    head_size, block_len, order_ref, x_ref, grad_ref, exact_ref, lse_ref, out_ref,
    rows_ref, near_ref, back_ref, key_ref, value_ref,
):
    total, width = x_ref.shape
    group = width // 3
    chunk = min(CHUNK, total)
    scale = head_size ** (-0.5)
    to_natural(order_ref, x_ref, rows_ref, block_len)
    to_natural(order_ref, grad_ref, near_ref, block_len)
    for head in range(group // head_size):
        spot = head * head_size
        for first in reversed(range(0, total, chunk)):
            last = first + chunk
            query = rows_ref[first:last, spot : spot + head_size] * jnp.bfloat16(scale)
            keys = rows_ref[:last, group + spot : group + spot + head_size]
            values = rows_ref[:last, 2 * group + spot : 2 * group + spot + head_size]
            grad = near_ref[first:last, spot : spot + head_size]
            exact = exact_ref[first:last, spot : spot + head_size]
            delta = jnp.sum(grad.astype(jnp.float32) * exact, axis=1, keepdims=True)
            scores = causal_scores(query, keys, first)
            probs = jnp.exp(scores - lse_ref[first:last, head : head + 1])
            grad_probs = lax.dot_general(
                grad, values, (((1,), (1,)), ((), ())), preferred_element_type=jnp.float32
            )
            grad_scores = (probs * (grad_probs - delta)).astype(jnp.bfloat16)
            grad_query = jnp.dot(grad_scores, keys, preferred_element_type=jnp.float32) * scale
            back_ref[first:last, spot : spot + head_size] = grad_query.astype(jnp.bfloat16)
            grad_keys = lax.dot_general(
                grad_scores, query, (((0,), (0,)), ((), ())), preferred_element_type=jnp.float32
            )
            grad_values = lax.dot_general(
                probs.astype(jnp.bfloat16), grad, (((0,), (0,)), ((), ())),
                preferred_element_type=jnp.float32,
            )
            if last == total:
                key_ref[...] = grad_keys
                value_ref[...] = grad_values
            else:
                key_ref[:last, :] += grad_keys
                value_ref[:last, :] += grad_values
        back_ref[:, group + spot : group + spot + head_size] = key_ref[...].astype(jnp.bfloat16)
        back_ref[:, 2 * group + spot : 2 * group + spot + head_size] = value_ref[...].astype(jnp.bfloat16)
    from_natural(order_ref, back_ref, out_ref, block_len)


def in_vmem():
    return pl.BlockSpec(memory_space=pltpu.VMEM)


def in_smem():
    return pl.BlockSpec(memory_space=pltpu.SMEM)


def attend(order, rows, head_size, block_len):
    total, width = rows.shape
    group = width // 3
    return pl.pallas_call(
        functools.partial(attend_kernel, head_size, block_len),
        out_shape=(
            jax.ShapeDtypeStruct((total, group), jnp.bfloat16),
            jax.ShapeDtypeStruct((total, group), jnp.float32),
            jax.ShapeDtypeStruct((total, 128), jnp.float32),
        ),
        in_specs=[in_smem(), in_vmem()],
        out_specs=(in_vmem(), in_vmem(), in_vmem()),
        scratch_shapes=[
            pltpu.VMEM((total, width), jnp.bfloat16),
            pltpu.VMEM((total, group), jnp.bfloat16),
        ],
        compiler_params=pltpu.CompilerParams(vmem_limit_bytes=40 * 1024 * 1024),
    )(order, rows)


def attend_back(order, rows, grad, exact, lse, head_size, block_len):
    total, width = rows.shape
    group = width // 3
    return pl.pallas_call(
        functools.partial(attend_back_kernel, head_size, block_len),
        out_shape=jax.ShapeDtypeStruct((total, width), jnp.bfloat16),
        in_specs=[in_smem(), in_vmem(), in_vmem(), in_vmem(), in_vmem()],
        out_specs=in_vmem(),
        scratch_shapes=[
            pltpu.VMEM((total, width), jnp.bfloat16),
            pltpu.VMEM((total, group), jnp.bfloat16),
            pltpu.VMEM((total, width), jnp.bfloat16),
            pltpu.VMEM((total, head_size), jnp.float32),
            pltpu.VMEM((total, head_size), jnp.float32),
        ],
        compiler_params=pltpu.CompilerParams(vmem_limit_bytes=48 * 1024 * 1024),
    )(order, rows, grad, exact, lse)


def spread_out(array, seq_count, groups, parts):
    row_count, width = array.shape[1], array.shape[2] // parts
    cut = array.reshape(seq_count, row_count, parts, groups, width // groups)
    cut = jnp.transpose(cut, (0, 3, 1, 2, 4))
    cut = cut.reshape(seq_count * groups, row_count, parts * (width // groups))
    moved = lax.all_to_all(cut, "ctx", 0, 0, tiled=True)
    return moved.reshape(seq_count * groups * row_count, parts * (width // groups))


def bring_back(array, seq_count, groups, parts):
    places = seq_count * groups
    row_count, width = array.shape[0] // places, array.shape[1] // parts
    moved = lax.all_to_all(array.reshape(places, row_count, parts * width), "ctx", 0, 0, tiled=True)
    cut = moved.reshape(seq_count, groups, row_count, parts, width)
    cut = jnp.transpose(cut, (0, 2, 3, 1, 4))
    return cut.reshape(seq_count, row_count, parts * groups * width)


def whole_weight(part):
    places = lax.axis_size("ctx")
    rows = part.shape[0]
    if rows % places:
        return lax.all_gather(part, "wsh", axis=0, tiled=True)
    share = rows // places
    own = lax.dynamic_slice_in_dim(part, lax.axis_index("ctx") * share, share, 0)
    return lax.all_gather(own, ("wsh", "ctx"), axis=0, tiled=True)


def owned_gradient(grad):
    places = lax.axis_size("ctx")
    near = grad.astype(jnp.bfloat16)
    if near.shape[0] % (places * lax.axis_size("wsh")):
        part = lax.psum_scatter(near, "wsh", scatter_dimension=0, tiled=True).astype(jnp.float32)
        return lax.psum(part, "ctx")
    part = lax.psum_scatter(near, ("wsh", "ctx"), scatter_dimension=0, tiled=True)
    return lax.all_gather(part, "ctx", axis=0, tiled=True).astype(jnp.float32)


def loop_attend(qkv, pair_of_device, block_len, qpos_low, qpos_up, scale):
    seq_count, row_count = qkv.shape[0], qkv.shape[1]
    model_width = qkv.shape[2] // 3
    head_count = HEADS
    head_size = model_width // head_count
    queries = qkv[..., :model_width].reshape(seq_count, row_count, head_count, head_size)
    query_low = queries[:, :block_len]
    query_up = queries[:, block_len:]
    kv_local = qkv[..., model_width:]

    def split_keys(slab_rows):
        keys = slab_rows[..., :model_width].reshape(seq_count, -1, head_count, head_size)
        values = slab_rows[..., model_width:].reshape(seq_count, -1, head_count, head_size)
        return (keys, values)

    empty_state = (
        jnp.zeros((seq_count, head_count, block_len, head_size), jnp.float32),
        jnp.full((seq_count, head_count, block_len), LOWEST, jnp.float32),
        jnp.zeros((seq_count, head_count, block_len), jnp.float32),
    )
    slab = lax.all_gather(kv_local, "ctx", axis=1, tiled=True)
    row_total = slab.shape[1]
    stride = math.gcd(row_total, max(row_count, 512))

    def turn(index, running):
        offset_row = index * stride
        sub_rows = lax.dynamic_slice_in_dim(slab, offset_row, stride, 1)
        key_pos = key_positions(
            offset_row + jnp.arange(stride, dtype=jnp.int32), pair_of_device, block_len
        )
        keys, values = split_keys(sub_rows)
        low_keys, low_values = split_keys(lower_rows(sub_rows, block_len))
        low_pos = lower_spots(key_pos, block_len)
        state_low = online_step(
            running[0], query_low, qpos_low, low_keys, low_values, low_pos, scale
        )
        state_up = online_step(running[1], query_up, qpos_up, keys, values, key_pos, scale)
        return (state_low, state_up)

    states = lax.fori_loop(0, row_total // stride, turn, (empty_state, empty_state))

    def finish(state):
        accum, top_score, total = state
        return (accum / total[..., None], top_score + jnp.log(total))

    attended_low, log_low = finish(states[0])
    attended_up, log_up = finish(states[1])
    attended = jnp.transpose(jnp.concatenate([attended_low, attended_up], axis=2), (0, 2, 1, 3))
    return attended, (query_low, query_up, kv_local, split_keys, log_low, log_up)


def loop_attend_back(kept, grad_heads, attended, pair_of_device, block_len, qpos_low, qpos_up, scale):
    query_low, query_up, kv_local, split_keys, log_low, log_up = kept
    seq_count, row_count, head_count, head_size = grad_heads.shape
    model_width = head_count * head_size
    grad_low = grad_heads[:, :block_len]
    grad_high = grad_heads[:, block_len:]
    delta = jnp.einsum("sqhd,sqhd->shq", grad_heads.astype(jnp.float32), attended)
    delta_low = delta[:, :, :block_len]
    delta_up = delta[:, :, block_len:]
    gathered = lax.all_gather(kv_local, "ctx", axis=1, tiled=True)
    total_rows = gathered.shape[1]

    def back_sub(sub_rows, first_row):
        stride = sub_rows.shape[1]
        key_pos = key_positions(
            first_row + jnp.arange(stride, dtype=jnp.int32), pair_of_device, block_len
        )
        keys, values = split_keys(sub_rows)
        low_keys, low_values = split_keys(lower_rows(sub_rows, block_len))
        low_pos = lower_spots(key_pos, block_len)
        probs_up, dscore_up = scores_back(
            query_up, qpos_up, log_up, delta_up, grad_high, keys, values, key_pos, scale
        )
        probs_low, dscore_low = scores_back(
            query_low, qpos_low, log_low, delta_low, grad_low, low_keys, low_values, low_pos, scale
        )
        return (keys, low_keys, probs_up, dscore_up, probs_low, dscore_low)

    def query_terms(parts):
        keys, low_keys, probs_up, dscore_up, probs_low, dscore_low = parts
        term_low = (
            jnp.einsum("shqk,skhd->sqhd", dscore_low, low_keys, preferred_element_type=jnp.float32)
            * scale
        )
        term_up = (
            jnp.einsum("shqk,skhd->sqhd", dscore_up, keys, preferred_element_type=jnp.float32)
            * scale
        )
        return (term_low, term_up)

    def key_value_terms(parts):
        keys, low_keys, probs_up, dscore_up, probs_low, dscore_low = parts
        stride = keys.shape[1]
        dkey_all = (
            jnp.einsum("shqk,sqhd->kshd", dscore_up, query_up, preferred_element_type=jnp.float32)
            * scale
        )
        dvalue_all = jnp.einsum(
            "shqk,sqhd->kshd", probs_up, grad_high, preferred_element_type=jnp.float32
        )
        dkey_low = (
            jnp.einsum("shqk,sqhd->kshd", dscore_low, query_low, preferred_element_type=jnp.float32)
            * scale
        )
        dvalue_low = jnp.einsum(
            "shqk,sqhd->kshd", probs_low, grad_low, preferred_element_type=jnp.float32
        )
        both_all = jnp.concatenate(
            [
                dkey_all.reshape(stride, seq_count, model_width),
                dvalue_all.reshape(stride, seq_count, model_width),
            ],
            axis=-1,
        )
        both_low = jnp.concatenate(
            [
                dkey_low.reshape(stride // 2, seq_count, model_width),
                dvalue_low.reshape(stride // 2, seq_count, model_width),
            ],
            axis=-1,
        )
        split_all = both_all.reshape(stride // row_count, 2, block_len, seq_count, 2 * model_width)
        merged = jnp.stack(
            [
                split_all[:, 0]
                + both_low.reshape(stride // row_count, block_len, seq_count, 2 * model_width),
                split_all[:, 1],
            ],
            axis=1,
        )
        return merged.reshape(stride, seq_count, 2 * model_width)

    zero_query = jnp.zeros((seq_count, block_len, head_count, head_size), jnp.float32)
    full_stride = math.gcd(total_rows, max(row_count, 512))

    def query_turn(index, running):
        first_row = index * full_stride
        sub_rows = lax.dynamic_slice_in_dim(gathered, first_row, full_stride, 1)
        term_low, term_up = query_terms(back_sub(sub_rows, first_row))
        return (running[0] + term_low, running[1] + term_up)

    dquery_low, dquery_up = lax.fori_loop(
        0, total_rows // full_stride, query_turn, (zero_query, zero_query)
    )
    row_total = row_count * lax.axis_size("ctx")
    key_stride = math.gcd(row_total, max(row_count, 512))

    def rows_turn(running, index):
        offset_row = index * key_stride
        sub_rows = lax.dynamic_slice_in_dim(gathered, offset_row, key_stride, 1)
        return (running, key_value_terms(back_sub(sub_rows, offset_row)))

    ignored, pieces = lax.scan(
        rows_turn, None, jnp.arange(row_total // key_stride, dtype=jnp.int32)
    )
    summed = lax.psum_scatter(
        pieces.reshape(row_total, seq_count, 2 * model_width),
        "ctx",
        scatter_dimension=0,
        tiled=True,
    )
    grad_kv = jnp.transpose(summed, (1, 0, 2)).astype(jnp.bfloat16)
    grad_query = (
        jnp.concatenate([dquery_low, dquery_up], axis=1)
        .reshape(seq_count, row_count, model_width)
        .astype(jnp.bfloat16)
    )
    return jnp.concatenate([grad_query, grad_kv], axis=-1)


def body(
    block_input,
    ln1_gain,
    ln1_bias,
    w_qkv,
    bias_query,
    bias_value,
    w_out,
    bias_out,
    ln2_gain,
    ln2_bias,
    w_up,
    bias_up,
    w_down,
    bias_down,
    pair_of_device,
    cotangent,
):
    small = (
        ln1_gain, ln1_bias, bias_query, bias_value, bias_out, ln2_gain, ln2_bias, bias_down, bias_up,
    )
    packed = lax.all_gather(jnp.concatenate(small).reshape(1, -1), "wsh", axis=0, tiled=True)
    packed = packed.astype(jnp.float32)
    whole_small = []
    start = 0
    for one in small:
        whole_small.append(packed[:, start : start + one.shape[0]].reshape(-1))
        start += one.shape[0]
    (
        gain_first,
        shift_first,
        query_shift,
        value_shift,
        out_shift,
        gain_second,
        shift_second,
        down_shift,
        up_shift,
    ) = whole_small
    whole_qkv = whole_weight(w_qkv)
    whole_out = whole_weight(w_out)
    whole_up = whole_weight(w_up)
    whole_down = whole_weight(w_down)
    seq_count, row_count, model_width = block_input.shape
    block_len = row_count // 2
    head_count = HEADS
    head_size = model_width // head_count
    scale = head_size ** (-0.5)
    places = lax.axis_size("ctx")
    own_index = lax.axis_index("ctx")
    own_pair = jnp.sum(
        jnp.where(jnp.arange(places, dtype=jnp.int32) == own_index, pair_of_device, 0)
    )
    offsets = jnp.arange(block_len, dtype=jnp.int32)
    qpos_low = own_pair * block_len + offsets
    qpos_up = (2 * places - 1 - own_pair) * block_len + offsets
    by_heads = places % seq_count == 0 and head_count % (places // seq_count) == 0
    inputs_f = block_input.astype(jnp.float32)
    normed_f, ln_one_back = jax.vjp(layer_norm, inputs_f, gain_first, shift_first)
    normed = normed_f.astype(jnp.bfloat16)
    qkv_shift = jnp.concatenate([query_shift, jnp.zeros_like(query_shift), value_shift])
    qkv = (jnp.dot(normed, whole_qkv, preferred_element_type=jnp.float32) + qkv_shift).astype(
        jnp.bfloat16
    )
    if by_heads:
        groups = places // seq_count
        blocks = jnp.arange(2 * places, dtype=jnp.int32)
        sought = jnp.minimum(blocks, 2 * places - 1 - blocks)
        hits = pair_of_device[None, :] == sought[:, None]
        holder = jnp.sum(jnp.where(hits, jnp.arange(places, dtype=jnp.int32)[None, :], 0), axis=1)
        order = 2 * holder + (blocks >= places).astype(jnp.int32)
        head_rows = spread_out(qkv, seq_count, groups, 3)
        mixed, exact, lse = attend(order, head_rows, head_size, block_len)
        attended_bf = bring_back(mixed, seq_count, groups, 1)
    else:
        attended, kept = loop_attend(
            qkv, pair_of_device, block_len, qpos_low, qpos_up, scale
        )
        attended_bf = attended.reshape(seq_count, row_count, model_width).astype(jnp.bfloat16)
    middle = (
        inputs_f + jnp.dot(attended_bf, whole_out, preferred_element_type=jnp.float32) + out_shift
    )
    normed_two_f, ln_two_back = jax.vjp(layer_norm, middle, gain_second, shift_second)
    normed_two = normed_two_f.astype(jnp.bfloat16)
    hidden = jnp.dot(normed_two, whole_up, preferred_element_type=jnp.float32) + up_shift
    active_f, gelu_back = jax.vjp(gelu_tanh, hidden)
    active = active_f.astype(jnp.bfloat16)
    output = (
        middle + jnp.dot(active, whole_down, preferred_element_type=jnp.float32) + down_shift
    ).astype(jnp.bfloat16)
    cotangent_f = cotangent.astype(jnp.float32)
    grad_down = jnp.einsum("srf,srd->fd", active, cotangent, preferred_element_type=jnp.float32)
    grad_bias_down = jnp.sum(cotangent_f, axis=(0, 1))
    grad_active = jnp.einsum(
        "srd,fd->srf", cotangent, whole_down, preferred_element_type=jnp.float32
    )
    grad_hidden = gelu_back(grad_active)[0].astype(jnp.bfloat16)
    grad_up = jnp.einsum("srd,srf->df", normed_two, grad_hidden, preferred_element_type=jnp.float32)
    grad_bias_up = jnp.sum(grad_hidden.astype(jnp.float32), axis=(0, 1))
    grad_normed_two = jnp.einsum(
        "srf,df->srd", grad_hidden, whole_up, preferred_element_type=jnp.float32
    )
    grad_middle_part, grad_ln2_gain, grad_ln2_bias = ln_two_back(grad_normed_two)
    grad_middle = cotangent_f + grad_middle_part
    grad_branch = grad_middle.astype(jnp.bfloat16)
    grad_out = jnp.einsum(
        "sri,sro->io", attended_bf, grad_branch, preferred_element_type=jnp.float32
    )
    grad_bias_out = jnp.sum(grad_branch.astype(jnp.float32), axis=(0, 1))
    grad_attended = jnp.einsum(
        "sro,io->sri", grad_branch, whole_out, preferred_element_type=jnp.float32
    ).astype(jnp.bfloat16)
    if by_heads:
        grad_back = spread_out(grad_attended, seq_count, groups, 1)
        grad_head_rows = attend_back(order, head_rows, grad_back, exact, lse, head_size, block_len)
        grad_rows = bring_back(grad_head_rows, seq_count, groups, 3)
    else:
        grad_rows = loop_attend_back(
            kept,
            grad_attended.reshape(seq_count, row_count, head_count, head_size),
            attended, pair_of_device, block_len, qpos_low, qpos_up, scale,
        )
    grad_qkv = jnp.einsum("srd,sre->de", normed, grad_rows, preferred_element_type=jnp.float32)
    row_sums = jnp.sum(grad_rows.astype(jnp.float32), axis=(0, 1))
    grad_bias_query = row_sums[:model_width]
    grad_bias_value = row_sums[2 * model_width :]
    grad_normed = jnp.einsum(
        "sre,de->srd", grad_rows, whole_qkv, preferred_element_type=jnp.float32
    )
    grad_input_part, grad_ln1_gain, grad_ln1_bias = ln_one_back(grad_normed)
    grad_input = grad_middle + grad_input_part
    vectors = (
        grad_ln1_gain, grad_ln1_bias, grad_bias_query, grad_bias_value, grad_bias_out,
        grad_ln2_gain, grad_ln2_bias, grad_bias_down, grad_bias_up,
    )
    shards = lax.axis_size("wsh")
    stacked = jnp.concatenate([one.reshape(shards, -1) for one in vectors], axis=1)
    summed = lax.psum(stacked, ("wsh", "ctx"))
    mine = lax.dynamic_slice_in_dim(summed, lax.axis_index("wsh"), 1, 0)[0]
    own = []
    start = 0
    for one in vectors:
        size = one.shape[0] // shards
        own.append(mine[start : start + size])
        start += size
    (
        own_ln1_gain, own_ln1_bias, own_bias_query, own_bias_value, own_bias_out,
        own_ln2_gain, own_ln2_bias, own_bias_down, own_bias_up,
    ) = own
    return (
        output,
        grad_input,
        own_ln1_gain,
        own_ln1_bias,
        owned_gradient(grad_qkv),
        own_bias_query,
        own_bias_value,
        owned_gradient(grad_out),
        own_bias_out,
        own_ln2_gain,
        own_ln2_bias,
        owned_gradient(grad_up),
        own_bias_up,
        owned_gradient(grad_down),
        own_bias_down,
    )


def solution(mesh):
    in_specs = (
        P("wsh", "ctx", None),
        P("wsh"),
        P("wsh"),
        P("wsh", None),
        P("wsh"),
        P("wsh"),
        P("wsh", None),
        P("wsh"),
        P("wsh"),
        P("wsh"),
        P("wsh", None),
        P("wsh"),
        P("wsh", None),
        P("wsh"),
        P(),
        P("wsh", "ctx", None),
    )
    out_specs = (
        P("wsh", "ctx", None),
        P("wsh", "ctx", None),
        P("wsh"),
        P("wsh"),
        P("wsh", None),
        P("wsh"),
        P("wsh"),
        P("wsh", None),
        P("wsh"),
        P("wsh"),
        P("wsh"),
        P("wsh", None),
        P("wsh"),
        P("wsh", None),
        P("wsh"),
    )
    return jax.shard_map(body, mesh=mesh, in_specs=in_specs, out_specs=out_specs, check_vma=False)
```

```python
import functools
import math

import jax
import jax.numpy as jnp
from jax import lax
from jax.experimental import pallas as pl
from jax.experimental.pallas import tpu as pltpu
from jax.sharding import PartitionSpec as P

HEADS = 12


EPSILON = 1e-05
MASKED = -1000000000.0
LOWEST = -1e30


def layer_norm(values, gain, shift):
    center = jnp.mean(values, axis=-1, keepdims=True)
    offset = values - center
    spread = jnp.mean(offset * offset, axis=-1, keepdims=True)
    return offset * lax.rsqrt(spread + EPSILON) * gain + shift


def gelu_tanh(values):
    return jax.nn.gelu(values, approximate=True)


def key_positions(row_index, pair_table, block_len):
    places = pair_table.shape[0]
    owner = row_index // (2 * block_len)
    inner = row_index % (2 * block_len)
    hits = owner[:, None] == jnp.arange(places, dtype=jnp.int32)[None, :]
    chosen = jnp.sum(jnp.where(hits, pair_table[None, :], 0), axis=1)
    which = jnp.where(inner < block_len, chosen, 2 * places - 1 - chosen)
    return which * block_len + inner % block_len


def lower_rows(array, block_len):
    seq_count, row_total, feature = array.shape
    paired = array.reshape(seq_count, row_total // (2 * block_len), 2, block_len, feature)
    return paired[:, :, 0].reshape(seq_count, row_total // 2, feature)


def lower_spots(spots, block_len):
    return spots.reshape(-1, 2, block_len)[:, 0].reshape(-1)


def online_step(state, query, query_pos, keys, values, key_pos, scale):
    accum, top_score, total = state
    scores = jnp.einsum("sqhd,skhd->shqk", query, keys, preferred_element_type=jnp.float32) * scale
    scores = jnp.where(
        key_pos[None, None, None, :] <= query_pos[None, None, :, None], scores, MASKED
    )
    new_top = jnp.maximum(top_score, jnp.max(scores, axis=-1))
    fading = jnp.exp(top_score - new_top)
    weights = jnp.exp(scores - new_top[..., None])
    total = total * fading + jnp.sum(weights, axis=-1)
    accum = accum * fading[..., None] + jnp.einsum(
        "shqk,skhd->shqd", weights.astype(jnp.bfloat16), values, preferred_element_type=jnp.float32
    )
    return (accum, new_top, total)


def scores_back(query, query_pos, log_total, delta, grad_head, keys, values, key_pos, scale):
    scores = jnp.einsum("sqhd,skhd->shqk", query, keys, preferred_element_type=jnp.float32) * scale
    scores = jnp.where(
        key_pos[None, None, None, :] <= query_pos[None, None, :, None], scores, MASKED
    )
    probs = jnp.exp(scores - log_total[..., None])
    grad_probs = jnp.einsum(
        "sqhd,skhd->shqk", grad_head, values, preferred_element_type=jnp.float32
    )
    grad_scores = (probs * (grad_probs - delta[..., None])).astype(jnp.bfloat16)
    return (probs.astype(jnp.bfloat16), grad_scores)


CHUNK = 256


def to_natural(order_ref, source_ref, target_ref, block_len):
    for block in range(source_ref.shape[0] // block_len):
        start = pl.multiple_of(order_ref[block] * block_len, block_len)
        target_ref[pl.ds(block * block_len, block_len), :] = source_ref[pl.ds(start, block_len), :]


def from_natural(order_ref, source_ref, target_ref, block_len):
    for block in range(source_ref.shape[0] // block_len):
        start = pl.multiple_of(order_ref[block] * block_len, block_len)
        target_ref[pl.ds(start, block_len), :] = source_ref[pl.ds(block * block_len, block_len), :]


def causal_scores(query, keys, first):
    scores = lax.dot_general(
        query, keys, (((1,), (1,)), ((), ())), preferred_element_type=jnp.float32
    )
    rows = lax.broadcasted_iota(jnp.int32, scores.shape, 0) + first
    columns = lax.broadcasted_iota(jnp.int32, scores.shape, 1)
    return jnp.where(columns <= rows, scores, MASKED)


def attend_kernel(head_size, block_len, order_ref, x_ref, out_ref, exact_ref, lse_ref, rows_ref, near_ref):
    total, width = x_ref.shape
    group = width // 3
    chunk = min(CHUNK, total)
    scale = head_size ** (-0.5)
    to_natural(order_ref, x_ref, rows_ref, block_len)
    for head in range(group // head_size):
        spot = head * head_size
        for first in range(0, total, chunk):
            last = first + chunk
            query = rows_ref[first:last, spot : spot + head_size] * jnp.bfloat16(scale)
            keys = rows_ref[:last, group + spot : group + spot + head_size]
            values = rows_ref[:last, 2 * group + spot : 2 * group + spot + head_size]
            scores = causal_scores(query, keys, first)
            top = jnp.max(scores, axis=1, keepdims=True)
            weights = jnp.exp(scores - top)
            amount = jnp.sum(weights, axis=1, keepdims=True)
            mixed = jnp.dot(
                weights.astype(jnp.bfloat16), values, preferred_element_type=jnp.float32
            ) * (1.0 / amount)
            exact_ref[first:last, spot : spot + head_size] = mixed
            near_ref[first:last, spot : spot + head_size] = mixed.astype(jnp.bfloat16)
            lse_ref[first:last, head : head + 1] = top + jnp.log(amount)
    from_natural(order_ref, near_ref, out_ref, block_len)


def attend_back_kernel(
    head_size, block_len, order_ref, x_ref, grad_ref, exact_ref, lse_ref, out_ref,
    rows_ref, near_ref, back_ref, key_ref, value_ref,
):
    total, width = x_ref.shape
    group = width // 3
    chunk = min(CHUNK, total)
    scale = head_size ** (-0.5)
    to_natural(order_ref, x_ref, rows_ref, block_len)
    to_natural(order_ref, grad_ref, near_ref, block_len)
    for head in range(group // head_size):
        spot = head * head_size
        for first in reversed(range(0, total, chunk)):
            last = first + chunk
            query = rows_ref[first:last, spot : spot + head_size] * jnp.bfloat16(scale)
            keys = rows_ref[:last, group + spot : group + spot + head_size]
            values = rows_ref[:last, 2 * group + spot : 2 * group + spot + head_size]
            grad = near_ref[first:last, spot : spot + head_size]
            exact = exact_ref[first:last, spot : spot + head_size]
            delta = jnp.sum(grad.astype(jnp.float32) * exact, axis=1, keepdims=True)
            scores = causal_scores(query, keys, first)
            probs = jnp.exp(scores - lse_ref[first:last, head : head + 1])
            grad_probs = lax.dot_general(
                grad, values, (((1,), (1,)), ((), ())), preferred_element_type=jnp.float32
            )
            grad_scores = (probs * (grad_probs - delta)).astype(jnp.bfloat16)
            grad_query = jnp.dot(grad_scores, keys, preferred_element_type=jnp.float32) * scale
            back_ref[first:last, spot : spot + head_size] = grad_query.astype(jnp.bfloat16)
            grad_keys = lax.dot_general(
                grad_scores, query, (((0,), (0,)), ((), ())), preferred_element_type=jnp.float32
            )
            grad_values = lax.dot_general(
                probs.astype(jnp.bfloat16), grad, (((0,), (0,)), ((), ())),
                preferred_element_type=jnp.float32,
            )
            if last == total:
                key_ref[...] = grad_keys
                value_ref[...] = grad_values
            else:
                key_ref[:last, :] += grad_keys
                value_ref[:last, :] += grad_values
        back_ref[:, group + spot : group + spot + head_size] = key_ref[...].astype(jnp.bfloat16)
        back_ref[:, 2 * group + spot : 2 * group + spot + head_size] = value_ref[...].astype(jnp.bfloat16)
    from_natural(order_ref, back_ref, out_ref, block_len)


def in_vmem():
    return pl.BlockSpec(memory_space=pltpu.VMEM)


def in_smem():
    return pl.BlockSpec(memory_space=pltpu.SMEM)


def attend(order, rows, head_size, block_len):
    total, width = rows.shape
    group = width // 3
    return pl.pallas_call(
        functools.partial(attend_kernel, head_size, block_len),
        out_shape=(
            jax.ShapeDtypeStruct((total, group), jnp.bfloat16),
            jax.ShapeDtypeStruct((total, group), jnp.float32),
            jax.ShapeDtypeStruct((total, 128), jnp.float32),
        ),
        in_specs=[in_smem(), in_vmem()],
        out_specs=(in_vmem(), in_vmem(), in_vmem()),
        scratch_shapes=[
            pltpu.VMEM((total, width), jnp.bfloat16),
            pltpu.VMEM((total, group), jnp.bfloat16),
        ],
        compiler_params=pltpu.CompilerParams(vmem_limit_bytes=40 * 1024 * 1024),
    )(order, rows)


def attend_back(order, rows, grad, exact, lse, head_size, block_len):
    total, width = rows.shape
    group = width // 3
    return pl.pallas_call(
        functools.partial(attend_back_kernel, head_size, block_len),
        out_shape=jax.ShapeDtypeStruct((total, width), jnp.bfloat16),
        in_specs=[in_smem(), in_vmem(), in_vmem(), in_vmem(), in_vmem()],
        out_specs=in_vmem(),
        scratch_shapes=[
            pltpu.VMEM((total, width), jnp.bfloat16),
            pltpu.VMEM((total, group), jnp.bfloat16),
            pltpu.VMEM((total, width), jnp.bfloat16),
            pltpu.VMEM((total, head_size), jnp.float32),
            pltpu.VMEM((total, head_size), jnp.float32),
        ],
        compiler_params=pltpu.CompilerParams(vmem_limit_bytes=48 * 1024 * 1024),
    )(order, rows, grad, exact, lse)


def spread_out(array, seq_count, groups, parts):
    row_count, width = array.shape[1], array.shape[2] // parts
    cut = array.reshape(seq_count, row_count, parts, groups, width // groups)
    cut = jnp.transpose(cut, (0, 3, 1, 2, 4))
    cut = cut.reshape(seq_count * groups, row_count, parts * (width // groups))
    moved = lax.all_to_all(cut, "ctx", 0, 0, tiled=True)
    return moved.reshape(seq_count * groups * row_count, parts * (width // groups))


def bring_back(array, seq_count, groups, parts):
    places = seq_count * groups
    row_count, width = array.shape[0] // places, array.shape[1] // parts
    moved = lax.all_to_all(array.reshape(places, row_count, parts * width), "ctx", 0, 0, tiled=True)
    cut = moved.reshape(seq_count, groups, row_count, parts, width)
    cut = jnp.transpose(cut, (0, 2, 3, 1, 4))
    return cut.reshape(seq_count, row_count, parts * groups * width)


def bit_count(size):
    return size.bit_length() - 1


def even_powers():
    return all((lax.axis_size(name) & (lax.axis_size(name) - 1)) == 0 for name in ("ctx", "wsh"))


def swap(array, axis_name, bit):
    flip = 1 << bit
    pairs = [(index, index ^ flip) for index in range(lax.axis_size(axis_name))]
    return lax.ppermute(array, axis_name, pairs)


def halve(array, axis_name, lead, bits, order):
    left = sorted(order, reverse=True)
    for bit in order:
        dim = lead + left.index(bit)
        mine = (lax.axis_index(axis_name) >> bit) & 1
        away = lax.dynamic_index_in_dim(array, 1 - mine, dim, keepdims=False)
        kept = lax.dynamic_index_in_dim(array, mine, dim, keepdims=False)
        came = swap(away, axis_name, bit)
        array = (kept.astype(jnp.float32) + came.astype(jnp.float32)).astype(array.dtype)
        left.remove(bit)
    return array


def double(array, axis_name, lead, order):
    held = []
    for bit in order:
        came = swap(array, axis_name, bit)
        held = sorted(held + [bit], reverse=True)
        first = ((lax.axis_index(axis_name) >> bit) & 1) == 0
        array = jnp.stack(
            [jnp.where(first, array, came), jnp.where(first, came, array)],
            axis=lead + held.index(bit),
        )
    return array


def bit_order(bits, turned):
    rest = list(range(1, bits))
    return [0] + (rest[::-1] if turned else rest)


def whole_weight(part, turned=False):
    places, shards = lax.axis_size("ctx"), lax.axis_size("wsh")
    rows = part.shape[0]
    if rows % (8 * places) or not even_powers():
        return lax.all_gather(part, "wsh", axis=0, tiled=True)
    share = rows // places
    own = lax.dynamic_slice_in_dim(part, lax.axis_index("ctx") * share, share, 0)
    z_bits = bit_count(shards)
    own = double(own, "wsh", 0, list(range(z_bits))[::-1])
    own = double(own, "ctx", z_bits, bit_order(bit_count(places), turned)[::-1])
    return own.reshape(shards * rows, part.shape[1])


def owned_gradient(grad, turned=False):
    places, shards = lax.axis_size("ctx"), lax.axis_size("wsh")
    near = grad.astype(jnp.bfloat16)
    rows, width = near.shape
    if rows % (8 * places * shards) or not even_powers():
        part = lax.psum_scatter(near, "wsh", scatter_dimension=0, tiled=True).astype(jnp.float32)
        return lax.psum(part, "ctx")
    z_bits, bits = bit_count(shards), bit_count(places)
    share = rows // (places * shards)
    near = near.reshape((2,) * (z_bits + bits) + (share, width))
    order = bit_order(bits, turned)
    near = halve(near, "ctx", z_bits, bits, order)
    near = halve(near, "wsh", 0, z_bits, list(range(z_bits)))
    near = double(near, "ctx", 0, order[::-1])
    return near.reshape(rows // shards, width).astype(jnp.float32)


def owned_vectors(stacked):
    if not even_powers():
        summed = lax.psum(stacked, ("wsh", "ctx"))
        return lax.dynamic_slice_in_dim(summed, lax.axis_index("wsh"), 1, 0)[0]
    z_bits = bit_count(lax.axis_size("wsh"))
    mine = stacked.reshape((2,) * z_bits + (1, stacked.shape[1]))
    mine = halve(mine, "wsh", 0, z_bits, list(range(z_bits)))
    for bit in range(bit_count(lax.axis_size("ctx"))):
        mine = mine + swap(mine, "ctx", bit)
    return mine[0]


def loop_attend(qkv, pair_of_device, block_len, qpos_low, qpos_up, scale):
    seq_count, row_count = qkv.shape[0], qkv.shape[1]
    model_width = qkv.shape[2] // 3
    head_count = HEADS
    head_size = model_width // head_count
    queries = qkv[..., :model_width].reshape(seq_count, row_count, head_count, head_size)
    query_low = queries[:, :block_len]
    query_up = queries[:, block_len:]
    kv_local = qkv[..., model_width:]

    def split_keys(slab_rows):
        keys = slab_rows[..., :model_width].reshape(seq_count, -1, head_count, head_size)
        values = slab_rows[..., model_width:].reshape(seq_count, -1, head_count, head_size)
        return (keys, values)

    empty_state = (
        jnp.zeros((seq_count, head_count, block_len, head_size), jnp.float32),
        jnp.full((seq_count, head_count, block_len), LOWEST, jnp.float32),
        jnp.zeros((seq_count, head_count, block_len), jnp.float32),
    )
    slab = lax.all_gather(kv_local, "ctx", axis=1, tiled=True)
    row_total = slab.shape[1]
    stride = math.gcd(row_total, max(row_count, 512))

    def turn(index, running):
        offset_row = index * stride
        sub_rows = lax.dynamic_slice_in_dim(slab, offset_row, stride, 1)
        key_pos = key_positions(
            offset_row + jnp.arange(stride, dtype=jnp.int32), pair_of_device, block_len
        )
        keys, values = split_keys(sub_rows)
        low_keys, low_values = split_keys(lower_rows(sub_rows, block_len))
        low_pos = lower_spots(key_pos, block_len)
        state_low = online_step(
            running[0], query_low, qpos_low, low_keys, low_values, low_pos, scale
        )
        state_up = online_step(running[1], query_up, qpos_up, keys, values, key_pos, scale)
        return (state_low, state_up)

    states = lax.fori_loop(0, row_total // stride, turn, (empty_state, empty_state))

    def finish(state):
        accum, top_score, total = state
        return (accum / total[..., None], top_score + jnp.log(total))

    attended_low, log_low = finish(states[0])
    attended_up, log_up = finish(states[1])
    attended = jnp.transpose(jnp.concatenate([attended_low, attended_up], axis=2), (0, 2, 1, 3))
    return attended, (query_low, query_up, kv_local, split_keys, log_low, log_up)


def loop_attend_back(kept, grad_heads, attended, pair_of_device, block_len, qpos_low, qpos_up, scale):
    query_low, query_up, kv_local, split_keys, log_low, log_up = kept
    seq_count, row_count, head_count, head_size = grad_heads.shape
    model_width = head_count * head_size
    grad_low = grad_heads[:, :block_len]
    grad_high = grad_heads[:, block_len:]
    delta = jnp.einsum("sqhd,sqhd->shq", grad_heads.astype(jnp.float32), attended)
    delta_low = delta[:, :, :block_len]
    delta_up = delta[:, :, block_len:]
    gathered = lax.all_gather(kv_local, "ctx", axis=1, tiled=True)
    total_rows = gathered.shape[1]

    def back_sub(sub_rows, first_row):
        stride = sub_rows.shape[1]
        key_pos = key_positions(
            first_row + jnp.arange(stride, dtype=jnp.int32), pair_of_device, block_len
        )
        keys, values = split_keys(sub_rows)
        low_keys, low_values = split_keys(lower_rows(sub_rows, block_len))
        low_pos = lower_spots(key_pos, block_len)
        probs_up, dscore_up = scores_back(
            query_up, qpos_up, log_up, delta_up, grad_high, keys, values, key_pos, scale
        )
        probs_low, dscore_low = scores_back(
            query_low, qpos_low, log_low, delta_low, grad_low, low_keys, low_values, low_pos, scale
        )
        return (keys, low_keys, probs_up, dscore_up, probs_low, dscore_low)

    def query_terms(parts):
        keys, low_keys, probs_up, dscore_up, probs_low, dscore_low = parts
        term_low = (
            jnp.einsum("shqk,skhd->sqhd", dscore_low, low_keys, preferred_element_type=jnp.float32)
            * scale
        )
        term_up = (
            jnp.einsum("shqk,skhd->sqhd", dscore_up, keys, preferred_element_type=jnp.float32)
            * scale
        )
        return (term_low, term_up)

    def key_value_terms(parts):
        keys, low_keys, probs_up, dscore_up, probs_low, dscore_low = parts
        stride = keys.shape[1]
        dkey_all = (
            jnp.einsum("shqk,sqhd->kshd", dscore_up, query_up, preferred_element_type=jnp.float32)
            * scale
        )
        dvalue_all = jnp.einsum(
            "shqk,sqhd->kshd", probs_up, grad_high, preferred_element_type=jnp.float32
        )
        dkey_low = (
            jnp.einsum("shqk,sqhd->kshd", dscore_low, query_low, preferred_element_type=jnp.float32)
            * scale
        )
        dvalue_low = jnp.einsum(
            "shqk,sqhd->kshd", probs_low, grad_low, preferred_element_type=jnp.float32
        )
        both_all = jnp.concatenate(
            [
                dkey_all.reshape(stride, seq_count, model_width),
                dvalue_all.reshape(stride, seq_count, model_width),
            ],
            axis=-1,
        )
        both_low = jnp.concatenate(
            [
                dkey_low.reshape(stride // 2, seq_count, model_width),
                dvalue_low.reshape(stride // 2, seq_count, model_width),
            ],
            axis=-1,
        )
        split_all = both_all.reshape(stride // row_count, 2, block_len, seq_count, 2 * model_width)
        merged = jnp.stack(
            [
                split_all[:, 0]
                + both_low.reshape(stride // row_count, block_len, seq_count, 2 * model_width),
                split_all[:, 1],
            ],
            axis=1,
        )
        return merged.reshape(stride, seq_count, 2 * model_width)

    zero_query = jnp.zeros((seq_count, block_len, head_count, head_size), jnp.float32)
    full_stride = math.gcd(total_rows, max(row_count, 512))

    def query_turn(index, running):
        first_row = index * full_stride
        sub_rows = lax.dynamic_slice_in_dim(gathered, first_row, full_stride, 1)
        term_low, term_up = query_terms(back_sub(sub_rows, first_row))
        return (running[0] + term_low, running[1] + term_up)

    dquery_low, dquery_up = lax.fori_loop(
        0, total_rows // full_stride, query_turn, (zero_query, zero_query)
    )
    row_total = row_count * lax.axis_size("ctx")
    key_stride = math.gcd(row_total, max(row_count, 512))

    def rows_turn(running, index):
        offset_row = index * key_stride
        sub_rows = lax.dynamic_slice_in_dim(gathered, offset_row, key_stride, 1)
        return (running, key_value_terms(back_sub(sub_rows, offset_row)))

    ignored, pieces = lax.scan(
        rows_turn, None, jnp.arange(row_total // key_stride, dtype=jnp.int32)
    )
    summed = lax.psum_scatter(
        pieces.reshape(row_total, seq_count, 2 * model_width),
        "ctx",
        scatter_dimension=0,
        tiled=True,
    )
    grad_kv = jnp.transpose(summed, (1, 0, 2)).astype(jnp.bfloat16)
    grad_query = (
        jnp.concatenate([dquery_low, dquery_up], axis=1)
        .reshape(seq_count, row_count, model_width)
        .astype(jnp.bfloat16)
    )
    return jnp.concatenate([grad_query, grad_kv], axis=-1)


def body(
    block_input,
    ln1_gain,
    ln1_bias,
    w_qkv,
    bias_query,
    bias_value,
    w_out,
    bias_out,
    ln2_gain,
    ln2_bias,
    w_up,
    bias_up,
    w_down,
    bias_down,
    pair_of_device,
    cotangent,
):
    small = (
        ln1_gain, ln1_bias, bias_query, bias_value, bias_out, ln2_gain, ln2_bias, bias_down, bias_up,
    )
    packed = lax.all_gather(jnp.concatenate(small).reshape(1, -1), "wsh", axis=0, tiled=True)
    packed = packed.astype(jnp.float32)
    whole_small = []
    start = 0
    for one in small:
        whole_small.append(packed[:, start : start + one.shape[0]].reshape(-1))
        start += one.shape[0]
    (
        gain_first,
        shift_first,
        query_shift,
        value_shift,
        out_shift,
        gain_second,
        shift_second,
        down_shift,
        up_shift,
    ) = whole_small
    half = w_qkv.shape[1] // 2
    whole_qkv = jnp.concatenate(
        [whole_weight(w_qkv[:, :half], True), whole_weight(w_qkv[:, half:])], axis=1
    )
    whole_out = whole_weight(w_out, True)
    whole_up = whole_weight(w_up)
    whole_down = whole_weight(w_down, True)
    seq_count, row_count, model_width = block_input.shape
    block_len = row_count // 2
    head_count = HEADS
    head_size = model_width // head_count
    scale = head_size ** (-0.5)
    places = lax.axis_size("ctx")
    own_index = lax.axis_index("ctx")
    own_pair = jnp.sum(
        jnp.where(jnp.arange(places, dtype=jnp.int32) == own_index, pair_of_device, 0)
    )
    offsets = jnp.arange(block_len, dtype=jnp.int32)
    qpos_low = own_pair * block_len + offsets
    qpos_up = (2 * places - 1 - own_pair) * block_len + offsets
    by_heads = places % seq_count == 0 and head_count % (places // seq_count) == 0
    inputs_f = block_input.astype(jnp.float32)
    normed_f, ln_one_back = jax.vjp(layer_norm, inputs_f, gain_first, shift_first)
    normed = normed_f.astype(jnp.bfloat16)
    qkv_shift = jnp.concatenate([query_shift, jnp.zeros_like(query_shift), value_shift])
    qkv = (jnp.dot(normed, whole_qkv, preferred_element_type=jnp.float32) + qkv_shift).astype(
        jnp.bfloat16
    )
    if by_heads:
        groups = places // seq_count
        blocks = jnp.arange(2 * places, dtype=jnp.int32)
        sought = jnp.minimum(blocks, 2 * places - 1 - blocks)
        hits = pair_of_device[None, :] == sought[:, None]
        holder = jnp.sum(jnp.where(hits, jnp.arange(places, dtype=jnp.int32)[None, :], 0), axis=1)
        order = 2 * holder + (blocks >= places).astype(jnp.int32)
        head_rows = spread_out(qkv, seq_count, groups, 3)
        mixed, exact, lse = attend(order, head_rows, head_size, block_len)
        attended_bf = bring_back(mixed, seq_count, groups, 1)
    else:
        attended, kept = loop_attend(
            qkv, pair_of_device, block_len, qpos_low, qpos_up, scale
        )
        attended_bf = attended.reshape(seq_count, row_count, model_width).astype(jnp.bfloat16)
    middle = (
        inputs_f + jnp.dot(attended_bf, whole_out, preferred_element_type=jnp.float32) + out_shift
    )
    normed_two_f, ln_two_back = jax.vjp(layer_norm, middle, gain_second, shift_second)
    normed_two = normed_two_f.astype(jnp.bfloat16)
    hidden = jnp.dot(normed_two, whole_up, preferred_element_type=jnp.float32) + up_shift
    active_f, gelu_back = jax.vjp(gelu_tanh, hidden)
    active = active_f.astype(jnp.bfloat16)
    output = (
        middle + jnp.dot(active, whole_down, preferred_element_type=jnp.float32) + down_shift
    ).astype(jnp.bfloat16)
    cotangent_f = cotangent.astype(jnp.float32)
    grad_down = jnp.einsum("srf,srd->fd", active, cotangent, preferred_element_type=jnp.float32)
    grad_bias_down = jnp.sum(cotangent_f, axis=(0, 1))
    grad_active = jnp.einsum(
        "srd,fd->srf", cotangent, whole_down, preferred_element_type=jnp.float32
    )
    grad_hidden = gelu_back(grad_active)[0].astype(jnp.bfloat16)
    grad_up = jnp.einsum("srd,srf->df", normed_two, grad_hidden, preferred_element_type=jnp.float32)
    grad_bias_up = jnp.sum(grad_hidden.astype(jnp.float32), axis=(0, 1))
    grad_normed_two = jnp.einsum(
        "srf,df->srd", grad_hidden, whole_up, preferred_element_type=jnp.float32
    )
    grad_middle_part, grad_ln2_gain, grad_ln2_bias = ln_two_back(grad_normed_two)
    grad_middle = cotangent_f + grad_middle_part
    grad_branch = grad_middle.astype(jnp.bfloat16)
    grad_out = jnp.einsum(
        "sri,sro->io", attended_bf, grad_branch, preferred_element_type=jnp.float32
    )
    grad_bias_out = jnp.sum(grad_branch.astype(jnp.float32), axis=(0, 1))
    grad_attended = jnp.einsum(
        "sro,io->sri", grad_branch, whole_out, preferred_element_type=jnp.float32
    ).astype(jnp.bfloat16)
    if by_heads:
        grad_back = spread_out(grad_attended, seq_count, groups, 1)
        grad_head_rows = attend_back(order, head_rows, grad_back, exact, lse, head_size, block_len)
        grad_rows = bring_back(grad_head_rows, seq_count, groups, 3)
    else:
        grad_rows = loop_attend_back(
            kept,
            grad_attended.reshape(seq_count, row_count, head_count, head_size),
            attended, pair_of_device, block_len, qpos_low, qpos_up, scale,
        )
    grad_qkv = jnp.einsum("srd,sre->de", normed, grad_rows, preferred_element_type=jnp.float32)
    row_sums = jnp.sum(grad_rows.astype(jnp.float32), axis=(0, 1))
    grad_bias_query = row_sums[:model_width]
    grad_bias_value = row_sums[2 * model_width :]
    grad_normed = jnp.einsum(
        "sre,de->srd", grad_rows, whole_qkv, preferred_element_type=jnp.float32
    )
    grad_input_part, grad_ln1_gain, grad_ln1_bias = ln_one_back(grad_normed)
    grad_input = grad_middle + grad_input_part
    vectors = (
        grad_ln1_gain, grad_ln1_bias, grad_bias_query, grad_bias_value, grad_bias_out,
        grad_ln2_gain, grad_ln2_bias, grad_bias_down, grad_bias_up,
    )
    shards = lax.axis_size("wsh")
    stacked = jnp.concatenate([one.reshape(shards, -1) for one in vectors], axis=1)
    mine = owned_vectors(stacked)
    own = []
    start = 0
    for one in vectors:
        size = one.shape[0] // shards
        own.append(mine[start : start + size])
        start += size
    (
        own_ln1_gain, own_ln1_bias, own_bias_query, own_bias_value, own_bias_out,
        own_ln2_gain, own_ln2_bias, own_bias_down, own_bias_up,
    ) = own
    return (
        output,
        grad_input,
        own_ln1_gain,
        own_ln1_bias,
        jnp.concatenate(
            [
                owned_gradient(grad_qkv[:, :half], True),
                owned_gradient(grad_qkv[:, half:]),
            ],
            axis=1,
        ),
        own_bias_query,
        own_bias_value,
        owned_gradient(grad_out, True),
        own_bias_out,
        own_ln2_gain,
        own_ln2_bias,
        owned_gradient(grad_up),
        own_bias_up,
        owned_gradient(grad_down, True),
        own_bias_down,
    )


def solution(mesh):
    in_specs = (
        P("wsh", "ctx", None),
        P("wsh"),
        P("wsh"),
        P("wsh", None),
        P("wsh"),
        P("wsh"),
        P("wsh", None),
        P("wsh"),
        P("wsh"),
        P("wsh"),
        P("wsh", None),
        P("wsh"),
        P("wsh", None),
        P("wsh"),
        P(),
        P("wsh", "ctx", None),
    )
    out_specs = (
        P("wsh", "ctx", None),
        P("wsh", "ctx", None),
        P("wsh"),
        P("wsh"),
        P("wsh", None),
        P("wsh"),
        P("wsh"),
        P("wsh", None),
        P("wsh"),
        P("wsh"),
        P("wsh"),
        P("wsh", None),
        P("wsh"),
        P("wsh", None),
        P("wsh"),
    )
    return jax.shard_map(body, mesh=mesh, in_specs=in_specs, out_specs=out_specs, check_vma=False)
```

```python
import functools
import math

import jax
import jax.numpy as jnp
from jax import lax
from jax.experimental import pallas as pl
from jax.experimental.pallas import tpu as pltpu
from jax.sharding import PartitionSpec as P

HEADS = 12


EPSILON = 1e-05
MASKED = -1000000000.0
LOWEST = -1e30


def layer_norm(values, gain, shift):
    center = jnp.mean(values, axis=-1, keepdims=True)
    offset = values - center
    spread = jnp.mean(offset * offset, axis=-1, keepdims=True)
    return offset * lax.rsqrt(spread + EPSILON) * gain + shift


def gelu_tanh(values):
    return jax.nn.gelu(values, approximate=True)


def key_positions(row_index, pair_table, block_len):
    places = pair_table.shape[0]
    owner = row_index // (2 * block_len)
    inner = row_index % (2 * block_len)
    hits = owner[:, None] == jnp.arange(places, dtype=jnp.int32)[None, :]
    chosen = jnp.sum(jnp.where(hits, pair_table[None, :], 0), axis=1)
    which = jnp.where(inner < block_len, chosen, 2 * places - 1 - chosen)
    return which * block_len + inner % block_len


def lower_rows(array, block_len):
    seq_count, row_total, feature = array.shape
    paired = array.reshape(seq_count, row_total // (2 * block_len), 2, block_len, feature)
    return paired[:, :, 0].reshape(seq_count, row_total // 2, feature)


def lower_spots(spots, block_len):
    return spots.reshape(-1, 2, block_len)[:, 0].reshape(-1)


def online_step(state, query, query_pos, keys, values, key_pos, scale):
    accum, top_score, total = state
    scores = jnp.einsum("sqhd,skhd->shqk", query, keys, preferred_element_type=jnp.float32) * scale
    scores = jnp.where(
        key_pos[None, None, None, :] <= query_pos[None, None, :, None], scores, MASKED
    )
    new_top = jnp.maximum(top_score, jnp.max(scores, axis=-1))
    fading = jnp.exp(top_score - new_top)
    weights = jnp.exp(scores - new_top[..., None])
    total = total * fading + jnp.sum(weights, axis=-1)
    accum = accum * fading[..., None] + jnp.einsum(
        "shqk,skhd->shqd", weights.astype(jnp.bfloat16), values, preferred_element_type=jnp.float32
    )
    return (accum, new_top, total)


def scores_back(query, query_pos, log_total, delta, grad_head, keys, values, key_pos, scale):
    scores = jnp.einsum("sqhd,skhd->shqk", query, keys, preferred_element_type=jnp.float32) * scale
    scores = jnp.where(
        key_pos[None, None, None, :] <= query_pos[None, None, :, None], scores, MASKED
    )
    probs = jnp.exp(scores - log_total[..., None])
    grad_probs = jnp.einsum(
        "sqhd,skhd->shqk", grad_head, values, preferred_element_type=jnp.float32
    )
    grad_scores = (probs * (grad_probs - delta[..., None])).astype(jnp.bfloat16)
    return (probs.astype(jnp.bfloat16), grad_scores)


CHUNK = 256


def to_natural(order_ref, source_ref, target_ref, block_len):
    for block in range(source_ref.shape[0] // block_len):
        start = pl.multiple_of(order_ref[block] * block_len, block_len)
        target_ref[pl.ds(block * block_len, block_len), :] = source_ref[pl.ds(start, block_len), :]


def from_natural(order_ref, source_ref, target_ref, block_len):
    for block in range(source_ref.shape[0] // block_len):
        start = pl.multiple_of(order_ref[block] * block_len, block_len)
        target_ref[pl.ds(start, block_len), :] = source_ref[pl.ds(block * block_len, block_len), :]


def causal_scores(query, keys, first):
    scores = lax.dot_general(
        query, keys, (((1,), (1,)), ((), ())), preferred_element_type=jnp.float32
    )
    rows = lax.broadcasted_iota(jnp.int32, scores.shape, 0) + first
    columns = lax.broadcasted_iota(jnp.int32, scores.shape, 1)
    return jnp.where(columns <= rows, scores, MASKED)


def attend_kernel(head_size, block_len, order_ref, x_ref, out_ref, exact_ref, lse_ref, rows_ref, near_ref):
    total, width = x_ref.shape
    group = width // 3
    chunk = min(CHUNK, total)
    scale = head_size ** (-0.5)
    to_natural(order_ref, x_ref, rows_ref, block_len)
    for head in range(group // head_size):
        spot = head * head_size
        for first in range(0, total, chunk):
            last = first + chunk
            query = rows_ref[first:last, spot : spot + head_size] * jnp.bfloat16(scale)
            keys = rows_ref[:last, group + spot : group + spot + head_size]
            values = rows_ref[:last, 2 * group + spot : 2 * group + spot + head_size]
            scores = causal_scores(query, keys, first)
            top = jnp.max(scores, axis=1, keepdims=True)
            weights = jnp.exp(scores - top)
            amount = jnp.sum(weights, axis=1, keepdims=True)
            mixed = jnp.dot(
                weights.astype(jnp.bfloat16), values, preferred_element_type=jnp.float32
            ) * (1.0 / amount)
            exact_ref[first:last, spot : spot + head_size] = mixed
            near_ref[first:last, spot : spot + head_size] = mixed.astype(jnp.bfloat16)
            lse_ref[first:last, head : head + 1] = top + jnp.log(amount)
    from_natural(order_ref, near_ref, out_ref, block_len)


def attend_back_kernel(
    head_size, block_len, order_ref, x_ref, grad_ref, exact_ref, lse_ref, out_ref,
    rows_ref, near_ref, back_ref, key_ref, value_ref,
):
    total, width = x_ref.shape
    group = width // 3
    chunk = min(CHUNK, total)
    scale = head_size ** (-0.5)
    to_natural(order_ref, x_ref, rows_ref, block_len)
    to_natural(order_ref, grad_ref, near_ref, block_len)
    for head in range(group // head_size):
        spot = head * head_size
        for first in reversed(range(0, total, chunk)):
            last = first + chunk
            query = rows_ref[first:last, spot : spot + head_size] * jnp.bfloat16(scale)
            keys = rows_ref[:last, group + spot : group + spot + head_size]
            values = rows_ref[:last, 2 * group + spot : 2 * group + spot + head_size]
            grad = near_ref[first:last, spot : spot + head_size]
            exact = exact_ref[first:last, spot : spot + head_size]
            delta = jnp.sum(grad.astype(jnp.float32) * exact, axis=1, keepdims=True)
            scores = causal_scores(query, keys, first)
            probs = jnp.exp(scores - lse_ref[first:last, head : head + 1])
            grad_probs = lax.dot_general(
                grad, values, (((1,), (1,)), ((), ())), preferred_element_type=jnp.float32
            )
            grad_scores = (probs * (grad_probs - delta)).astype(jnp.bfloat16)
            grad_query = jnp.dot(grad_scores, keys, preferred_element_type=jnp.float32) * scale
            back_ref[first:last, spot : spot + head_size] = grad_query.astype(jnp.bfloat16)
            grad_keys = lax.dot_general(
                grad_scores, query, (((0,), (0,)), ((), ())), preferred_element_type=jnp.float32
            )
            grad_values = lax.dot_general(
                probs.astype(jnp.bfloat16), grad, (((0,), (0,)), ((), ())),
                preferred_element_type=jnp.float32,
            )
            if last == total:
                key_ref[...] = grad_keys
                value_ref[...] = grad_values
            else:
                key_ref[:last, :] += grad_keys
                value_ref[:last, :] += grad_values
        back_ref[:, group + spot : group + spot + head_size] = key_ref[...].astype(jnp.bfloat16)
        back_ref[:, 2 * group + spot : 2 * group + spot + head_size] = value_ref[...].astype(jnp.bfloat16)
    from_natural(order_ref, back_ref, out_ref, block_len)


def in_vmem():
    return pl.BlockSpec(memory_space=pltpu.VMEM)


def in_smem():
    return pl.BlockSpec(memory_space=pltpu.SMEM)


def attend(order, rows, head_size, block_len):
    total, width = rows.shape
    group = width // 3
    return pl.pallas_call(
        functools.partial(attend_kernel, head_size, block_len),
        out_shape=(
            jax.ShapeDtypeStruct((total, group), jnp.bfloat16),
            jax.ShapeDtypeStruct((total, group), jnp.float32),
            jax.ShapeDtypeStruct((total, 128), jnp.float32),
        ),
        in_specs=[in_smem(), in_vmem()],
        out_specs=(in_vmem(), in_vmem(), in_vmem()),
        scratch_shapes=[
            pltpu.VMEM((total, width), jnp.bfloat16),
            pltpu.VMEM((total, group), jnp.bfloat16),
        ],
        compiler_params=pltpu.CompilerParams(vmem_limit_bytes=40 * 1024 * 1024),
    )(order, rows)


def attend_back(order, rows, grad, exact, lse, head_size, block_len):
    total, width = rows.shape
    group = width // 3
    return pl.pallas_call(
        functools.partial(attend_back_kernel, head_size, block_len),
        out_shape=jax.ShapeDtypeStruct((total, width), jnp.bfloat16),
        in_specs=[in_smem(), in_vmem(), in_vmem(), in_vmem(), in_vmem()],
        out_specs=in_vmem(),
        scratch_shapes=[
            pltpu.VMEM((total, width), jnp.bfloat16),
            pltpu.VMEM((total, group), jnp.bfloat16),
            pltpu.VMEM((total, width), jnp.bfloat16),
            pltpu.VMEM((total, head_size), jnp.float32),
            pltpu.VMEM((total, head_size), jnp.float32),
        ],
        compiler_params=pltpu.CompilerParams(vmem_limit_bytes=48 * 1024 * 1024),
    )(order, rows, grad, exact, lse)


def spread_out(array, seq_count, groups, parts):
    row_count, width = array.shape[1], array.shape[2] // parts
    cut = array.reshape(seq_count, row_count, parts, groups, width // groups)
    cut = jnp.transpose(cut, (0, 3, 1, 2, 4))
    cut = cut.reshape(seq_count * groups, row_count, parts * (width // groups))
    moved = lax.all_to_all(cut, "ctx", 0, 0, tiled=True)
    return moved.reshape(seq_count * groups * row_count, parts * (width // groups))


def bring_back(array, seq_count, groups, parts):
    places = seq_count * groups
    row_count, width = array.shape[0] // places, array.shape[1] // parts
    moved = lax.all_to_all(array.reshape(places, row_count, parts * width), "ctx", 0, 0, tiled=True)
    cut = moved.reshape(seq_count, groups, row_count, parts, width)
    cut = jnp.transpose(cut, (0, 2, 3, 1, 4))
    return cut.reshape(seq_count, row_count, parts * groups * width)


def bit_count(size):
    return size.bit_length() - 1


def even_powers():
    return all((lax.axis_size(name) & (lax.axis_size(name) - 1)) == 0 for name in ("ctx", "wsh"))


def swap(array, axis_name, bit):
    flip = 1 << bit
    pairs = [(index, index ^ flip) for index in range(lax.axis_size(axis_name))]
    return lax.ppermute(array, axis_name, pairs)


def halve(array, axis_name, lead, present, order):
    left = sorted(present, reverse=True)
    for bit in order:
        dim = lead + left.index(bit)
        mine = (lax.axis_index(axis_name) >> bit) & 1
        away = lax.dynamic_index_in_dim(array, 1 - mine, dim, keepdims=False)
        kept = lax.dynamic_index_in_dim(array, mine, dim, keepdims=False)
        came = swap(away, axis_name, bit)
        array = (kept.astype(jnp.float32) + came.astype(jnp.float32)).astype(array.dtype)
        left.remove(bit)
    return array


def double(array, axis_name, lead, order):
    held = []
    for bit in order:
        came = swap(array, axis_name, bit)
        held = sorted(held + [bit], reverse=True)
        first = ((lax.axis_index(axis_name) >> bit) & 1) == 0
        array = jnp.stack(
            [jnp.where(first, array, came), jnp.where(first, came, array)],
            axis=lead + held.index(bit),
        )
    return array


def bit_order(bits, turned):
    rest = list(range(1, bits))
    return [0] + (rest[::-1] if turned else rest)


def whole_weight(part, turned=False):
    places, shards = lax.axis_size("ctx"), lax.axis_size("wsh")
    rows = part.shape[0]
    if rows % (8 * places) or not even_powers():
        return lax.all_gather(part, "wsh", axis=0, tiled=True)
    share = rows // places
    own = lax.dynamic_slice_in_dim(part, lax.axis_index("ctx") * share, share, 0)
    z_bits = bit_count(shards)
    own = double(own, "wsh", 0, list(range(z_bits))[::-1])
    own = double(own, "ctx", z_bits, bit_order(bit_count(places), turned)[::-1])
    return own.reshape(shards * rows, part.shape[1])


def owned_gradient(grad, turned=False):
    places, shards = lax.axis_size("ctx"), lax.axis_size("wsh")
    near = grad.astype(jnp.bfloat16)
    rows, width = near.shape
    if rows % (8 * places * shards) or not even_powers():
        part = lax.psum_scatter(near, "wsh", scatter_dimension=0, tiled=True).astype(jnp.float32)
        return lax.psum(part, "ctx")
    z_bits, bits = bit_count(shards), bit_count(places)
    share = rows // (places * shards)
    near = near.reshape((2,) * (z_bits + bits) + (share, width))
    order = bit_order(bits, turned)
    near = halve(near, "ctx", z_bits, order, order)
    return finish_sum(near, order)


def can_stage(grad):
    places, shards = lax.axis_size("ctx"), lax.axis_size("wsh")
    return even_powers() and places >= 8 and grad.shape[0] % (8 * places * shards) == 0


def start_sum(grad, order):
    places, shards = lax.axis_size("ctx"), lax.axis_size("wsh")
    z_bits = bit_count(shards)
    share = grad.shape[0] // (places * shards)
    near = grad.astype(jnp.bfloat16)
    near = near.reshape((2,) * (z_bits + len(order)) + (share, grad.shape[1]))
    return halve(near, "ctx", z_bits, order, order[:1])


def more_sum(near, order, first, last):
    return halve(near, "ctx", bit_count(lax.axis_size("wsh")), order[first:], order[first:last])


def finish_sum(near, order):
    z_bits = bit_count(lax.axis_size("wsh"))
    near = halve(near, "wsh", 0, range(z_bits), list(range(z_bits)))
    near = double(near, "ctx", 0, order[::-1])
    return near.reshape(-1, near.shape[-1]).astype(jnp.float32)


def owned_vectors(stacked):
    if not even_powers():
        summed = lax.psum(stacked, ("wsh", "ctx"))
        return lax.dynamic_slice_in_dim(summed, lax.axis_index("wsh"), 1, 0)[0]
    z_bits = bit_count(lax.axis_size("wsh"))
    mine = stacked.reshape((2,) * z_bits + (1, stacked.shape[1]))
    mine = halve(mine, "wsh", 0, range(z_bits), list(range(z_bits)))
    for bit in range(bit_count(lax.axis_size("ctx"))):
        mine = mine + swap(mine, "ctx", bit)
    return mine[0]


def loop_attend(qkv, pair_of_device, block_len, qpos_low, qpos_up, scale):
    seq_count, row_count = qkv.shape[0], qkv.shape[1]
    model_width = qkv.shape[2] // 3
    head_count = HEADS
    head_size = model_width // head_count
    queries = qkv[..., :model_width].reshape(seq_count, row_count, head_count, head_size)
    query_low = queries[:, :block_len]
    query_up = queries[:, block_len:]
    kv_local = qkv[..., model_width:]

    def split_keys(slab_rows):
        keys = slab_rows[..., :model_width].reshape(seq_count, -1, head_count, head_size)
        values = slab_rows[..., model_width:].reshape(seq_count, -1, head_count, head_size)
        return (keys, values)

    empty_state = (
        jnp.zeros((seq_count, head_count, block_len, head_size), jnp.float32),
        jnp.full((seq_count, head_count, block_len), LOWEST, jnp.float32),
        jnp.zeros((seq_count, head_count, block_len), jnp.float32),
    )
    slab = lax.all_gather(kv_local, "ctx", axis=1, tiled=True)
    row_total = slab.shape[1]
    stride = math.gcd(row_total, max(row_count, 512))

    def turn(index, running):
        offset_row = index * stride
        sub_rows = lax.dynamic_slice_in_dim(slab, offset_row, stride, 1)
        key_pos = key_positions(
            offset_row + jnp.arange(stride, dtype=jnp.int32), pair_of_device, block_len
        )
        keys, values = split_keys(sub_rows)
        low_keys, low_values = split_keys(lower_rows(sub_rows, block_len))
        low_pos = lower_spots(key_pos, block_len)
        state_low = online_step(
            running[0], query_low, qpos_low, low_keys, low_values, low_pos, scale
        )
        state_up = online_step(running[1], query_up, qpos_up, keys, values, key_pos, scale)
        return (state_low, state_up)

    states = lax.fori_loop(0, row_total // stride, turn, (empty_state, empty_state))

    def finish(state):
        accum, top_score, total = state
        return (accum / total[..., None], top_score + jnp.log(total))

    attended_low, log_low = finish(states[0])
    attended_up, log_up = finish(states[1])
    attended = jnp.transpose(jnp.concatenate([attended_low, attended_up], axis=2), (0, 2, 1, 3))
    return attended, (query_low, query_up, kv_local, split_keys, log_low, log_up)


def loop_attend_back(kept, grad_heads, attended, pair_of_device, block_len, qpos_low, qpos_up, scale):
    query_low, query_up, kv_local, split_keys, log_low, log_up = kept
    seq_count, row_count, head_count, head_size = grad_heads.shape
    model_width = head_count * head_size
    grad_low = grad_heads[:, :block_len]
    grad_high = grad_heads[:, block_len:]
    delta = jnp.einsum("sqhd,sqhd->shq", grad_heads.astype(jnp.float32), attended)
    delta_low = delta[:, :, :block_len]
    delta_up = delta[:, :, block_len:]
    gathered = lax.all_gather(kv_local, "ctx", axis=1, tiled=True)
    total_rows = gathered.shape[1]

    def back_sub(sub_rows, first_row):
        stride = sub_rows.shape[1]
        key_pos = key_positions(
            first_row + jnp.arange(stride, dtype=jnp.int32), pair_of_device, block_len
        )
        keys, values = split_keys(sub_rows)
        low_keys, low_values = split_keys(lower_rows(sub_rows, block_len))
        low_pos = lower_spots(key_pos, block_len)
        probs_up, dscore_up = scores_back(
            query_up, qpos_up, log_up, delta_up, grad_high, keys, values, key_pos, scale
        )
        probs_low, dscore_low = scores_back(
            query_low, qpos_low, log_low, delta_low, grad_low, low_keys, low_values, low_pos, scale
        )
        return (keys, low_keys, probs_up, dscore_up, probs_low, dscore_low)

    def query_terms(parts):
        keys, low_keys, probs_up, dscore_up, probs_low, dscore_low = parts
        term_low = (
            jnp.einsum("shqk,skhd->sqhd", dscore_low, low_keys, preferred_element_type=jnp.float32)
            * scale
        )
        term_up = (
            jnp.einsum("shqk,skhd->sqhd", dscore_up, keys, preferred_element_type=jnp.float32)
            * scale
        )
        return (term_low, term_up)

    def key_value_terms(parts):
        keys, low_keys, probs_up, dscore_up, probs_low, dscore_low = parts
        stride = keys.shape[1]
        dkey_all = (
            jnp.einsum("shqk,sqhd->kshd", dscore_up, query_up, preferred_element_type=jnp.float32)
            * scale
        )
        dvalue_all = jnp.einsum(
            "shqk,sqhd->kshd", probs_up, grad_high, preferred_element_type=jnp.float32
        )
        dkey_low = (
            jnp.einsum("shqk,sqhd->kshd", dscore_low, query_low, preferred_element_type=jnp.float32)
            * scale
        )
        dvalue_low = jnp.einsum(
            "shqk,sqhd->kshd", probs_low, grad_low, preferred_element_type=jnp.float32
        )
        both_all = jnp.concatenate(
            [
                dkey_all.reshape(stride, seq_count, model_width),
                dvalue_all.reshape(stride, seq_count, model_width),
            ],
            axis=-1,
        )
        both_low = jnp.concatenate(
            [
                dkey_low.reshape(stride // 2, seq_count, model_width),
                dvalue_low.reshape(stride // 2, seq_count, model_width),
            ],
            axis=-1,
        )
        split_all = both_all.reshape(stride // row_count, 2, block_len, seq_count, 2 * model_width)
        merged = jnp.stack(
            [
                split_all[:, 0]
                + both_low.reshape(stride // row_count, block_len, seq_count, 2 * model_width),
                split_all[:, 1],
            ],
            axis=1,
        )
        return merged.reshape(stride, seq_count, 2 * model_width)

    zero_query = jnp.zeros((seq_count, block_len, head_count, head_size), jnp.float32)
    full_stride = math.gcd(total_rows, max(row_count, 512))

    def query_turn(index, running):
        first_row = index * full_stride
        sub_rows = lax.dynamic_slice_in_dim(gathered, first_row, full_stride, 1)
        term_low, term_up = query_terms(back_sub(sub_rows, first_row))
        return (running[0] + term_low, running[1] + term_up)

    dquery_low, dquery_up = lax.fori_loop(
        0, total_rows // full_stride, query_turn, (zero_query, zero_query)
    )
    row_total = row_count * lax.axis_size("ctx")
    key_stride = math.gcd(row_total, max(row_count, 512))

    def rows_turn(running, index):
        offset_row = index * key_stride
        sub_rows = lax.dynamic_slice_in_dim(gathered, offset_row, key_stride, 1)
        return (running, key_value_terms(back_sub(sub_rows, offset_row)))

    ignored, pieces = lax.scan(
        rows_turn, None, jnp.arange(row_total // key_stride, dtype=jnp.int32)
    )
    summed = lax.psum_scatter(
        pieces.reshape(row_total, seq_count, 2 * model_width),
        "ctx",
        scatter_dimension=0,
        tiled=True,
    )
    grad_kv = jnp.transpose(summed, (1, 0, 2)).astype(jnp.bfloat16)
    grad_query = (
        jnp.concatenate([dquery_low, dquery_up], axis=1)
        .reshape(seq_count, row_count, model_width)
        .astype(jnp.bfloat16)
    )
    return jnp.concatenate([grad_query, grad_kv], axis=-1)


def body(
    block_input,
    ln1_gain,
    ln1_bias,
    w_qkv,
    bias_query,
    bias_value,
    w_out,
    bias_out,
    ln2_gain,
    ln2_bias,
    w_up,
    bias_up,
    w_down,
    bias_down,
    pair_of_device,
    cotangent,
):
    small = (
        ln1_gain, ln1_bias, bias_query, bias_value, bias_out, ln2_gain, ln2_bias, bias_down, bias_up,
    )
    packed = lax.all_gather(jnp.concatenate(small).reshape(1, -1), "wsh", axis=0, tiled=True)
    packed = packed.astype(jnp.float32)
    whole_small = []
    start = 0
    for one in small:
        whole_small.append(packed[:, start : start + one.shape[0]].reshape(-1))
        start += one.shape[0]
    (
        gain_first,
        shift_first,
        query_shift,
        value_shift,
        out_shift,
        gain_second,
        shift_second,
        down_shift,
        up_shift,
    ) = whole_small
    half = w_qkv.shape[1] // 2
    whole_qkv = jnp.concatenate(
        [whole_weight(w_qkv[:, :half], True), whole_weight(w_qkv[:, half:])], axis=1
    )
    whole_out = whole_weight(w_out, True)
    whole_up = whole_weight(w_up)
    whole_down = whole_weight(w_down, True)
    seq_count, row_count, model_width = block_input.shape
    block_len = row_count // 2
    head_count = HEADS
    head_size = model_width // head_count
    scale = head_size ** (-0.5)
    places = lax.axis_size("ctx")
    own_index = lax.axis_index("ctx")
    own_pair = jnp.sum(
        jnp.where(jnp.arange(places, dtype=jnp.int32) == own_index, pair_of_device, 0)
    )
    offsets = jnp.arange(block_len, dtype=jnp.int32)
    qpos_low = own_pair * block_len + offsets
    qpos_up = (2 * places - 1 - own_pair) * block_len + offsets
    by_heads = places % seq_count == 0 and head_count % (places // seq_count) == 0
    inputs_f = block_input.astype(jnp.float32)
    normed_f, ln_one_back = jax.vjp(layer_norm, inputs_f, gain_first, shift_first)
    normed = normed_f.astype(jnp.bfloat16)
    qkv_shift = jnp.concatenate([query_shift, jnp.zeros_like(query_shift), value_shift])
    qkv = (jnp.dot(normed, whole_qkv, preferred_element_type=jnp.float32) + qkv_shift).astype(
        jnp.bfloat16
    )
    if by_heads:
        groups = places // seq_count
        blocks = jnp.arange(2 * places, dtype=jnp.int32)
        sought = jnp.minimum(blocks, 2 * places - 1 - blocks)
        hits = pair_of_device[None, :] == sought[:, None]
        holder = jnp.sum(jnp.where(hits, jnp.arange(places, dtype=jnp.int32)[None, :], 0), axis=1)
        order = 2 * holder + (blocks >= places).astype(jnp.int32)
        head_rows = spread_out(qkv, seq_count, groups, 3)
        mixed, exact, lse = attend(order, head_rows, head_size, block_len)
        attended_bf = bring_back(mixed, seq_count, groups, 1)
    else:
        attended, kept = loop_attend(
            qkv, pair_of_device, block_len, qpos_low, qpos_up, scale
        )
        attended_bf = attended.reshape(seq_count, row_count, model_width).astype(jnp.bfloat16)
    middle = (
        inputs_f + jnp.dot(attended_bf, whole_out, preferred_element_type=jnp.float32) + out_shift
    )
    normed_two_f, ln_two_back = jax.vjp(layer_norm, middle, gain_second, shift_second)
    normed_two = normed_two_f.astype(jnp.bfloat16)
    hidden = jnp.dot(normed_two, whole_up, preferred_element_type=jnp.float32) + up_shift
    active_f, gelu_back = jax.vjp(gelu_tanh, hidden)
    active = active_f.astype(jnp.bfloat16)
    output = (
        middle + jnp.dot(active, whole_down, preferred_element_type=jnp.float32) + down_shift
    ).astype(jnp.bfloat16)
    cotangent_f = cotangent.astype(jnp.float32)
    grad_down = jnp.einsum("srf,srd->fd", active, cotangent, preferred_element_type=jnp.float32)
    grad_bias_down = jnp.sum(cotangent_f, axis=(0, 1))
    grad_active = jnp.einsum(
        "srd,fd->srf", cotangent, whole_down, preferred_element_type=jnp.float32
    )
    grad_hidden = gelu_back(grad_active)[0].astype(jnp.bfloat16)
    grad_up = jnp.einsum("srd,srf->df", normed_two, grad_hidden, preferred_element_type=jnp.float32)
    grad_bias_up = jnp.sum(grad_hidden.astype(jnp.float32), axis=(0, 1))
    grad_normed_two = jnp.einsum(
        "srf,df->srd", grad_hidden, whole_up, preferred_element_type=jnp.float32
    )
    grad_middle_part, grad_ln2_gain, grad_ln2_bias = ln_two_back(grad_normed_two)
    grad_middle = cotangent_f + grad_middle_part
    grad_branch = grad_middle.astype(jnp.bfloat16)
    grad_out = jnp.einsum(
        "sri,sro->io", attended_bf, grad_branch, preferred_element_type=jnp.float32
    )
    grad_bias_out = jnp.sum(grad_branch.astype(jnp.float32), axis=(0, 1))
    grad_attended = jnp.einsum(
        "sro,io->sri", grad_branch, whole_out, preferred_element_type=jnp.float32
    ).astype(jnp.bfloat16)
    staged = by_heads and can_stage(grad_up) and can_stage(grad_down)
    if staged:
        up_order = bit_order(bit_count(places), False)
        down_order = bit_order(bit_count(places), True)
        grad_attended, part_up, part_down = lax.optimization_barrier(
            (grad_attended, start_sum(grad_up, up_order), start_sum(grad_down, down_order))
        )
    if by_heads:
        grad_back = spread_out(grad_attended, seq_count, groups, 1)
        grad_head_rows = attend_back(order, head_rows, grad_back, exact, lse, head_size, block_len)
        if staged:
            part_up = more_sum(part_up, up_order, 1, 2)
            part_down = more_sum(part_down, down_order, 1, 2)
            grad_head_rows, part_up, part_down = lax.optimization_barrier(
                (grad_head_rows, part_up, part_down)
            )
        grad_rows = bring_back(grad_head_rows, seq_count, groups, 3)
    else:
        grad_rows = loop_attend_back(
            kept,
            grad_attended.reshape(seq_count, row_count, head_count, head_size),
            attended, pair_of_device, block_len, qpos_low, qpos_up, scale,
        )
    grad_qkv = jnp.einsum("srd,sre->de", normed, grad_rows, preferred_element_type=jnp.float32)
    row_sums = jnp.sum(grad_rows.astype(jnp.float32), axis=(0, 1))
    grad_bias_query = row_sums[:model_width]
    grad_bias_value = row_sums[2 * model_width :]
    grad_normed = jnp.einsum(
        "sre,de->srd", grad_rows, whole_qkv, preferred_element_type=jnp.float32
    )
    grad_input_part, grad_ln1_gain, grad_ln1_bias = ln_one_back(grad_normed)
    grad_input = grad_middle + grad_input_part
    if staged:
        own_up = finish_sum(more_sum(part_up, up_order, 2, len(up_order)), up_order)
        own_down = finish_sum(more_sum(part_down, down_order, 2, len(down_order)), down_order)
    else:
        own_up = owned_gradient(grad_up)
        own_down = owned_gradient(grad_down, True)
    vectors = (
        grad_ln1_gain, grad_ln1_bias, grad_bias_query, grad_bias_value, grad_bias_out,
        grad_ln2_gain, grad_ln2_bias, grad_bias_down, grad_bias_up,
    )
    shards = lax.axis_size("wsh")
    stacked = jnp.concatenate([one.reshape(shards, -1) for one in vectors], axis=1)
    mine = owned_vectors(stacked)
    own = []
    start = 0
    for one in vectors:
        size = one.shape[0] // shards
        own.append(mine[start : start + size])
        start += size
    (
        own_ln1_gain, own_ln1_bias, own_bias_query, own_bias_value, own_bias_out,
        own_ln2_gain, own_ln2_bias, own_bias_down, own_bias_up,
    ) = own
    return (
        output,
        grad_input,
        own_ln1_gain,
        own_ln1_bias,
        jnp.concatenate(
            [
                owned_gradient(grad_qkv[:, :half], True),
                owned_gradient(grad_qkv[:, half:]),
            ],
            axis=1,
        ),
        own_bias_query,
        own_bias_value,
        owned_gradient(grad_out, True),
        own_bias_out,
        own_ln2_gain,
        own_ln2_bias,
        own_up,
        own_bias_up,
        own_down,
        own_bias_down,
    )


def solution(mesh):
    in_specs = (
        P("wsh", "ctx", None),
        P("wsh"),
        P("wsh"),
        P("wsh", None),
        P("wsh"),
        P("wsh"),
        P("wsh", None),
        P("wsh"),
        P("wsh"),
        P("wsh"),
        P("wsh", None),
        P("wsh"),
        P("wsh", None),
        P("wsh"),
        P(),
        P("wsh", "ctx", None),
    )
    out_specs = (
        P("wsh", "ctx", None),
        P("wsh", "ctx", None),
        P("wsh"),
        P("wsh"),
        P("wsh", None),
        P("wsh"),
        P("wsh"),
        P("wsh", None),
        P("wsh"),
        P("wsh"),
        P("wsh"),
        P("wsh", None),
        P("wsh"),
        P("wsh", None),
        P("wsh"),
    )
    return jax.shard_map(body, mesh=mesh, in_specs=in_specs, out_specs=out_specs, check_vma=False)
```
